32 devices in a mesh: sec: 2 (over x), tile: 16 (over z, y, core).
Axes of the slice: x: 2, y: 2, z: 4, core: 2. Of those that a mesh axis runs over, the one named last changes fastest.
Arguments:
- prognostic_quantities: float32 [5, 128, 512, 256], P(None, None, 'tile', 'sec'), may hold values from -6 to 6
- advective_ratio: float32 [2, 128], replicated, may hold values from -0.35 to 0.35
- horizontal_diffuse_ratio: float32 [128], replicated, may hold values from 0.08 to 0.16
- upright_diffuse_ratio: float32 [128], replicated, may hold values from 0.03 to 0.15
- transfer_coefficient: float32 [512, 256], P('tile', 'sec'), may hold values from 0.05 to 0.3
- terrain_outer_warmth: float32 [512, 256], P('tile', 'sec'), may hold values from -6 to 6
- earlier_marine_warmth: float32 [512, 256], P('tile', 'sec'), may hold values from -6 to 6
- marine_indicator: int32 [512, 256], P('tile', 'sec'), may hold values 0 or 1
- marine_salinity_heat_vector: float32 [2, 80, 32768], P(None, None, ('sec', 'tile')), may hold values from -6 to 6
- marine_layer_diffuse_ratio: float32 [79], replicated, may hold values from 0.3 to 3
- group_active_extent: int32 [32], P(('sec', 'tile')), may hold values from 1 to 1024, 16384 in all
- intersect_air_site: int32 [4, 32768], P(None, ('sec', 'tile')), may hold values from 0 to 12287, as said below
- intersect_interpolation_share: float32 [4, 32768], P(None, ('sec', 'tile')), may hold values from 0.1 to 0.5
Outputs:
- new_tracers: float32 [5, 128, 512, 256], P(None, None, 'tile', 'sec')
- resolved_marine_properties: float32 [2, 80, 32768], P(None, None, ('sec', 'tile'))
- upcoming_marine_warmth: float32 [512, 256], P('tile', 'sec')
The draws below stay inside these ranges and needn't reach their ends.
Inputs may be any that keep to these rules, and one draw needn't show every extreme that they name: `intersect_air_site`: in the columns of block b, entries below 4096 name a cell of tile b - 1, entries from 4096 to 8191 a cell of tile b, the rest a cell of tile b + 1; block 0 never names tile -1 and block 31 never names tile 32. Each block has 1024 column slots, of which the first group_active_extent are live; both ocean outputs are zero in the other slots, and some block is full.
All inputs are finite; a program needn't handle non-finite values. No bound on the sum of `marine_indicator` on one device may be relied on, other than what follows from the above.
Results may differ from the reference program's by a relative error of at most 0.00002.
Values sent between devices are 32-bit elements; how exact they have to be, the bound alone decides.
A program may use at most 192 MiB of HBM per device.

```python
import math
import jax
import jax.numpy as jnp
import numpy as np
from jax import lax

AY = 32
AX = 128
L = 128
OL = 80
NV = 5
STEPS = 3
K = 4
OCAP = 1024
NBLOCK = 32
CELLS = 4096
MESH_HEIGHT_Y = 512
MESH_WIDTH_X = 256
N_SEC = 2
N_TILE = 16


def draw_intersect_air_site(key, part):
    key_offset = jax.random.fold_in(key, 11)
    key_cell = jax.random.fold_in(key, 23)
    columns = NBLOCK * OCAP
    offset_pick = jax.random.randint(key_offset, (K, columns), 0, 4)
    offset = jnp.where(offset_pick == 0, -1, jnp.where(offset_pick == 3, 1, 0))
    block_index = jnp.arange(columns, dtype=jnp.int32) // OCAP
    offset = jnp.where((block_index[None, :] == 0) & (offset < 0), 0, offset)
    offset = jnp.where((block_index[None, :] == NBLOCK - 1) & (offset > 0), 0, offset)
    cell_index = jax.random.randint(key_cell, (K, columns), 0, CELLS)
    result = (offset + 1) * CELLS + cell_index
    result = result.at[0, 0].set(3 * CELLS - 1)
    result = result.at[0, OCAP].set(0)
    return result.astype(jnp.int32)


def set_ends(entries, rng, least, top_value):
    spot = [jax.random.randint(jax.random.fold_in(rng, axis), (), 0, length) for axis, length in enumerate(entries.shape)]
    longest = entries.shape.index(max(entries.shape))
    neighbour = spot[:longest] + [(spot[longest] + 1) % entries.shape[longest]] + spot[longest + 1:]
    return entries.at[tuple(spot)].set(least).at[tuple(neighbour)].set(top_value)


def block_scale(key, shape, shards, low, largest):
    level, own = 1.0, jax.random.fold_in(key, 6)
    for axis_at, shards_of in shards:
        steps = jnp.exp(jax.random.uniform(jax.random.fold_in(own, axis_at), (shards_of,), jnp.float32, low / len(shards), largest / len(shards)))
        level = level * jnp.repeat(steps, shape[axis_at] // shards_of).reshape([-1 if axis == axis_at else 1 for axis in range(len(shape))])
    return level


def profile(count, total, bound, lean):
    weights = [(1 << 20) // math.isqrt(standing ** lean) + 1 for standing in range(2, count + 1)]
    surplus, holding = total - bound - (count - 1), [1] * (count - 1)
    while surplus > 0:
        candidates = [i for i in range(count - 1) if holding[i] < bound]
        mass, left = sum([weights[i] for i in candidates]), surplus
        for i in candidates:
            extra = min(bound - holding[i], max(1, left * weights[i] // mass), surplus)
            holding[i] = holding[i] + extra
            surplus = surplus - extra
    return np.array([bound] + holding)


def ragged(rng, count, total, bound, slope):
    if count == 2:
        one = jax.random.randint(rng, (), max(1, total - bound), min(bound, total - 1) + 1)
        return jnp.stack([one, total - one])
    tallies = jnp.asarray(profile(count, total, bound, slope), jnp.int32)
    couples = (count - 1) // 2
    source_of, receiver = tallies[1:1 + 2 * couples:2], tallies[2:2 + 2 * couples:2]
    room = jnp.minimum(source_of - 1, bound - receiver)
    shifted = jax.random.randint(jax.random.fold_in(rng, 1), (couples,), 0, 1 << 20) % (room + 1)
    tallies = tallies.at[1:1 + 2 * couples:2].set(source_of - shifted).at[2:2 + 2 * couples:2].set(receiver + shifted)
    return tallies[jax.random.permutation(jax.random.fold_in(rng, 2), count)]


def normal_values(key, shape, width, bound, pieces=(), kind=jnp.bfloat16):
    array = jax.random.normal(key, shape, jnp.float32) * width
    if len(pieces) > 0:
        array = block_scale(key, shape, pieces, -0.22, 0.18) * array
    return jnp.clip(array, min=-bound, max=bound).astype(kind)


def setup_inputs(seed: int = 0) -> dict:
    arg_keys = jax.random.split(jax.random.key(seed), 14)
    return {
        "prognostic_quantities": normal_values(arg_keys[0], (NV, L, MESH_HEIGHT_Y, MESH_WIDTH_X), 1.0, 6.0, ((2, 16), (3, 2)), jnp.float32),
        "advective_ratio": jnp.clip(jax.random.uniform(arg_keys[1], (2, L), jnp.float32, -0.35, 0.35), -0.35, 0.35),
        "horizontal_diffuse_ratio": jnp.clip(jnp.exp(jax.random.uniform(arg_keys[2], (L,), jnp.float32, math.log(0.08), math.log(0.16))), 0.08, 0.16),
        "upright_diffuse_ratio": jnp.clip(jnp.exp(jax.random.uniform(arg_keys[3], (L,), jnp.float32, math.log(0.03), math.log(0.15))), 0.03, 0.15),
        "transfer_coefficient": jnp.clip(jnp.exp(math.log(0.3) - 1.7917595 * jax.random.uniform(arg_keys[4], (MESH_HEIGHT_Y, MESH_WIDTH_X), jnp.float32) ** block_scale(arg_keys[4], (MESH_HEIGHT_Y, MESH_WIDTH_X), ((0, 16), (1, 2)), -0.2, 0.2)), 0.05, 0.3),
        "terrain_outer_warmth": normal_values(arg_keys[5], (MESH_HEIGHT_Y, MESH_WIDTH_X), 1.0, 6.0, ((0, 16), (1, 2)), jnp.float32),
        "earlier_marine_warmth": normal_values(arg_keys[6], (MESH_HEIGHT_Y, MESH_WIDTH_X), 1.0, 6.0, ((0, 16), (1, 2)), jnp.float32),
        "marine_indicator": set_ends((jax.random.randint(arg_keys[7], (MESH_HEIGHT_Y, MESH_WIDTH_X), 0, 3) < 2).astype(jnp.int32), jax.random.fold_in(arg_keys[7], 1), 0, 1),
        "marine_salinity_heat_vector": normal_values(arg_keys[8], (2, OL, NBLOCK * OCAP), 1.0, 6.0, ((2, 32),), jnp.float32),
        "marine_layer_diffuse_ratio": jnp.clip(jnp.exp(jax.random.uniform(arg_keys[9], (OL - 1,), jnp.float32, math.log(0.3), math.log(3.0))), 0.3, 3.0),
        "group_active_extent": ragged(arg_keys[10], NBLOCK, NBLOCK * OCAP // 2, OCAP, 2).astype(jnp.int32),
        "intersect_air_site": draw_intersect_air_site(jax.random.fold_in(arg_keys[13], 71), 0),
        "intersect_interpolation_share": jnp.clip(0.1 + 0.4 * jax.random.uniform(arg_keys[12], (K, NBLOCK * OCAP), jnp.float32) ** block_scale(arg_keys[12], (K, NBLOCK * OCAP), ((1, 32),), -0.2, 0.2), 0.1, 0.5),
    }


def march_forward(margin_extended, advective_ratio, horizontal_diffuse_ratio, upright_diffuse_ratio, transfer_coefficient, outer_warmth, humid_multiplier):
    quantity_matrices = margin_extended[:, :, 1:-1, 1:-1]
    north_cells = margin_extended[:, :, 2:, 1:-1]
    south_cells = margin_extended[:, :, :-2, 1:-1]
    east_cells = margin_extended[:, :, 1:-1, 2:]
    west_cells = margin_extended[:, :, 1:-1, :-2]
    east_west = advective_ratio[0][None, :, None, None]
    north_south = advective_ratio[1][None, :, None, None]
    spread = east_cells + west_cells + north_cells + south_cells - 4.0 * quantity_matrices
    carried = 0.5 * east_west * (east_cells - west_cells) + 0.5 * north_south * (north_cells - south_cells)
    level_above = jnp.concatenate([quantity_matrices[:, :1], quantity_matrices[:, :-1]], axis=1)
    level_below = jnp.concatenate([quantity_matrices[:, 1:], quantity_matrices[:, -1:]], axis=1)
    mixing = upright_diffuse_ratio[None, :, None, None] * (level_above + level_below - 2.0 * quantity_matrices)
    updated = quantity_matrices + horizontal_diffuse_ratio[None, :, None, None] * spread - carried + mixing
    floor_index = quantity_matrices[:, -1]
    thermal_transfer = transfer_coefficient * (outer_warmth - floor_index[0])
    humidity_transfer = transfer_coefficient * humid_multiplier * (0.6 * outer_warmth - floor_index[1])
    surface = jnp.stack([thermal_transfer, humidity_transfer, jnp.zeros_like(thermal_transfer), -transfer_coefficient * floor_index[3], -transfer_coefficient * floor_index[4]])
    updated = jnp.concatenate([updated[:, :-1], updated[:, -1:] + surface[:, None]], axis=1)
    return (updated, thermal_transfer, humidity_transfer)

def tile_major(grid):
    return grid.reshape(N_TILE, AY, N_SEC, AX).transpose(2, 0, 1, 3).reshape(N_SEC * N_TILE * AY * AX)

def mesh_sorted(flat):
    return flat.reshape(N_SEC, N_TILE, AY, AX).transpose(1, 2, 0, 3).reshape(N_TILE * AY, N_SEC * AX)

def tridiagonal(marine_layer_diffuse_ratio):
    zero_one = jnp.zeros((1,), marine_layer_diffuse_ratio.dtype)
    upper_mix = jnp.concatenate([marine_layer_diffuse_ratio, zero_one])
    lower_mix = jnp.concatenate([zero_one, marine_layer_diffuse_ratio])
    return (-lower_mix, 1.0 + upper_mix + lower_mix, -upper_mix)

def reference(prognostic_quantities, advective_ratio, horizontal_diffuse_ratio, upright_diffuse_ratio, transfer_coefficient, terrain_outer_warmth, earlier_marine_warmth, marine_indicator, marine_salinity_heat_vector, marine_layer_diffuse_ratio, group_active_extent, intersect_air_site, intersect_interpolation_share):
    marine_share = marine_indicator.astype(jnp.float32)
    outer_warmth = marine_share * earlier_marine_warmth + (1.0 - marine_share) * terrain_outer_warmth
    humid_multiplier = 0.3 + 0.7 * marine_share
    quantity_matrices = prognostic_quantities
    heat_total = jnp.zeros_like(transfer_coefficient)
    moist_total = jnp.zeros_like(transfer_coefficient)
    for repeat in range(STEPS):
        margin_extended = jnp.pad(quantity_matrices, ((0, 0), (0, 0), (1, 1), (1, 1)))
        quantity_matrices, thermal_transfer, humidity_transfer = march_forward(margin_extended, advective_ratio, horizontal_diffuse_ratio, upright_diffuse_ratio, transfer_coefficient, outer_warmth, humid_multiplier)
        heat_total = heat_total + thermal_transfer
        moist_total = moist_total + humidity_transfer
    flux_flat = jnp.stack([tile_major(heat_total), tile_major(moist_total)])
    columns = NBLOCK * OCAP
    block_index = (jnp.arange(columns) // OCAP).astype(jnp.int32)
    slot_index = (jnp.arange(columns) % OCAP).astype(jnp.int32)
    flat_index = (block_index[None, :] * CELLS + intersect_air_site - CELLS).astype(jnp.int32)
    picked = flux_flat[:, flat_index]
    forcing = jnp.sum(picked * intersect_interpolation_share[None], axis=1)
    right_side = marine_salinity_heat_vector.at[0, 0].add(-0.5 * forcing[0]).at[1, 0].add(0.5 * forcing[1])
    lower_diag, main_diag, upper_diag = tridiagonal(marine_layer_diffuse_ratio)
    solved = lax.linalg.tridiagonal_solve(jnp.broadcast_to(lower_diag, (2, OL)), jnp.broadcast_to(main_diag, (2, OL)), jnp.broadcast_to(upper_diag, (2, OL)), right_side)
    live_slot = (slot_index < group_active_extent[block_index]).astype(jnp.float32)
    resolved_marine_properties = solved * live_slot[None, None]
    top_temp = resolved_marine_properties[0, 0]
    weighted = intersect_interpolation_share * live_slot[None]
    contrib_values = jnp.stack([weighted * top_temp[None], weighted]).reshape(2, -1)
    gathered_entries = jnp.zeros((2, NBLOCK * CELLS), jnp.float32).at[:, flat_index.reshape(-1)].add(contrib_values)
    upcoming_marine_warmth = (mesh_sorted(gathered_entries[0]) + earlier_marine_warmth) / (mesh_sorted(gathered_entries[1]) + 1.0)
    return (quantity_matrices, resolved_marine_properties, upcoming_marine_warmth)
```

```python
import functools

import jax
import jax.numpy as jnp
from jax import lax
from jax.experimental import pallas as pl
from jax.experimental.pallas import tpu as pltpu
from jax.sharding import PartitionSpec as P

STEPS = 3
HALO = STEPS
WINDOW = 2 * HALO
GROUPS = ((0, 2), (2, 3), (3, 5))
VMEM_LIMIT = 48 * 1024 * 1024


def call(kernel, **kwargs):
    return pl.pallas_call(
        kernel,
        compiler_params=pltpu.CompilerParams(vmem_limit_bytes=VMEM_LIMIT),
        **kwargs,
    )


SMEM = pl.BlockSpec(memory_space=pltpu.SMEM)
VMEM = pl.BlockSpec(memory_space=pltpu.VMEM)


def to_neighbours(low_edge, high_edge, axis):
    count = lax.axis_size(axis)
    forward = [(i, i + 1) for i in range(count - 1)]
    backward = [(i + 1, i) for i in range(count - 1)]
    return lax.ppermute(high_edge, axis, forward), lax.ppermute(low_edge, axis, backward)


def ring_halo(below, above):
    gap = jnp.zeros(above.shape[:-2] + (8 - 2 * HALO, above.shape[-1]), above.dtype)
    return jnp.concatenate([above, gap, below], axis=-2)


def pack_kernel(sec_ref, x_ref, surface_ref, o_ref):
    step = pl.program_id(0)
    kinds, quarters, chunk, rows, lanes = x_ref.shape
    base = jnp.where(sec_ref[0] == 0, 128 - (128 - HALO), HALO)
    first = jnp.where(sec_ref[0] == 0, 0, HALO)
    lane = lax.broadcasted_iota(jnp.int32, (rows, lanes), 1)

    def placed(block, slot, total):
        at = 32 * slot[0] + WINDOW * slot[1]
        moved = pltpu.roll(block, lax.rem(base + at, 128), 1)
        inside = (lane >= at + first) & (lane < at + first + HALO)
        return jnp.where(inside, moved, total)

    def body(i, carry):
        total = jnp.zeros((rows, lanes), jnp.float32)
        for q in range(quarters):
            for v in range(kinds):
                total = placed(x_ref[v, q, i], (q, v), total)
        o_ref[step * chunk + i] = total
        return carry

    lax.fori_loop(0, chunk, body, 0, unroll=4)

    @pl.when(step == 0)
    def _():
        total = jnp.zeros((rows, lanes), jnp.float32)
        for q in range(2):
            for v in range(kinds):
                total = placed(surface_ref[q, v], (q, v), total)
        o_ref[o_ref.shape[0] - 1] = total


def window_kernel(own_ref, other_ref, own_halo_ref, other_halo_ref, coef_ref, mask_ref, h_ref):
    depth = h_ref.shape[1]
    rows = own_ref.shape[1]
    h_ref[0, :, :rows] = own_ref[:depth] + other_ref[:depth]
    h_ref[0, :, rows:] = own_halo_ref[:depth] + other_halo_ref[:depth]
    surface = jnp.concatenate(
        [
            own_ref[depth] + other_ref[depth],
            own_halo_ref[depth] + other_halo_ref[depth],
        ],
        axis=0,
    )
    lane = lax.broadcasted_iota(jnp.int32, surface.shape, 1)
    bottom = lane >= 96
    add_const = jnp.where(bottom, pltpu.roll(surface, 96, 1), 0.0)
    add_slope = jnp.where(bottom, pltpu.roll(surface, 64, 1), 0.0)
    ring = surface.shape[0]
    for s in range(STEPS - 1):

        def update(kk, above, below):
            f = h_ref[s, kk]
            c = [coef_ref[kk, pl.ds(n, 1), :] for n in range(6)]
            new = (
                c[0] * f
                + c[1] * pltpu.roll(f, 127, 1)
                + c[2] * pltpu.roll(f, 1, 1)
                + c[3] * pltpu.roll(f, ring - 1, 0)
                + c[4] * pltpu.roll(f, 1, 0)
                + c[5] * (above + below)
            )
            return f, new

        def store(kk, new):
            h_ref[s + 1, kk] = new * mask_ref[...]

        top, last = h_ref[s, 0], h_ref[s, depth - 1]
        _, new = update(0, jnp.where(lane < 32, top, pltpu.roll(last, 32, 1)), h_ref[s, 1])
        store(0, new)

        def body(kk, carry):
            _, new = update(kk, h_ref[s, kk - 1], h_ref[s, kk + 1])
            store(kk, new)
            return carry

        lax.fori_loop(1, depth - 1, body, 0, unroll=True)
        f, new = update(
            depth - 1, h_ref[s, depth - 2], jnp.where(bottom, last, pltpu.roll(top, 96, 1))
        )
        store(depth - 1, new + (add_const - add_slope * f))


def march_kernel(
    with_flux, first_kind, sec_ref, x_ref, halo_ref, surface_ref, surface_halo_ref, h_ref,
    coef_ref, mask_ref, *rest
):
    if with_flux:
        out_ref, flux_ref, s0, s1 = rest
    else:
        _, out_ref, s0, s1 = rest
    kind = pl.program_id(0) + first_kind
    levels, rows = x_ref.shape[1:3]
    quarter = levels // 4
    ring = s0.shape[1]
    s0[:, :rows] = x_ref[0]
    s0[:, rows:] = halo_ref[0]
    is_west = sec_ref[0] == 0
    source = jnp.where(is_west, HALO, HALO - 1) + WINDOW * kind
    goal = jnp.where(is_west, 127, 0)
    halo_mask = mask_ref[pl.ds(rows, ring - rows), :]
    flux = None
    states = (s0, s1, s0)
    for s in range(STEPS):
        src = states[s]
        for q in range(4):
            shift = lax.rem(goal + 256 - source - 32 * q, 128)

            def body(kk, carry, src=src, q=q, shift=shift, s=s):
                k = q * quarter + kk
                f = src[k]
                above = src[jnp.maximum(k - 1, 0)]
                below = src[jnp.minimum(k + 1, levels - 1)]
                c = [coef_ref[k, pl.ds(n, 1), :] for n in range(7)]
                north = pltpu.roll(f, ring - 1, 0)
                south = pltpu.roll(f, 1, 0)
                beside = h_ref[s, kk]
                if s == STEPS - 1:
                    f, above, below, north, south, beside = (
                        a[:rows] for a in (f, above, below, north, south, beside)
                    )
                new = (
                    c[0] * f
                    + c[1] * pltpu.roll(f, 127, 1)
                    + c[2] * pltpu.roll(f, 1, 1)
                    + c[6] * pltpu.roll(beside, shift, 1)
                    + c[3] * north
                    + c[4] * south
                    + c[5] * (above + below)
                )
                if s == STEPS - 1:
                    out_ref[0, k] = new
                else:
                    dst = states[s + 1]
                    dst[k, pl.ds(0, rows), :] = new[:rows]
                    dst[k, pl.ds(rows, ring - rows), :] = new[rows:] * halo_mask
                return carry

            lax.fori_loop(0, quarter, body, 0, unroll=True)
        last = src[levels - 1]
        term = surface_ref[0, 0] - surface_ref[1, 0] * last[:rows]
        if s == STEPS - 1:
            out_ref[0, levels - 1] += term
        else:
            dst = states[s + 1]
            dst[levels - 1, pl.ds(0, rows), :] += term
            dst[levels - 1, pl.ds(rows, ring - rows), :] += halo_mask * (
                surface_halo_ref[0, 0] - surface_halo_ref[1, 0] * last[rows:]
            )
        flux = term if flux is None else flux + term
    if with_flux:
        flux_ref[0] = flux


def march(group, sec, fields, halo, surface, surface_halo, seam, coef, mask, written):
    start, stop = group
    kinds, levels, rows, lanes = fields.shape
    with_flux = written is None
    ring = rows + 8
    in_specs = [
        SMEM,
        pl.BlockSpec((1, levels, rows, lanes), lambda v: (v + start, 0, 0, 0)),
        pl.BlockSpec((1, levels, 8, lanes), lambda v: (v + start, 0, 0, 0)),
        pl.BlockSpec((2, 1, rows, lanes), lambda v: (0, v + start, 0, 0)),
        pl.BlockSpec((2, 1, 8, lanes), lambda v: (0, v + start, 0, 0)),
        VMEM,
        VMEM,
        VMEM,
    ]
    operands = [sec, fields, halo, surface, surface_halo, seam, coef, mask]
    out_specs = [pl.BlockSpec((1, levels, rows, lanes), lambda v: (v + start, 0, 0, 0))]
    out_shape = [jax.ShapeDtypeStruct(fields.shape, jnp.float32)]
    aliases = {}
    if with_flux:
        out_specs.append(pl.BlockSpec((1, rows, lanes), lambda v: (v, 0, 0)))
        out_shape.append(jax.ShapeDtypeStruct((stop - start, rows, lanes), jnp.float32))
    else:
        in_specs.append(pl.BlockSpec(memory_space=pl.ANY))
        operands.append(written)
        aliases = {len(operands) - 1: 0}
    count = (stop - start) * levels * rows * lanes
    return pl.pallas_call(
        functools.partial(march_kernel, with_flux, start),
        grid=(stop - start,),
        in_specs=in_specs,
        out_specs=out_specs,
        out_shape=out_shape,
        scratch_shapes=[pltpu.VMEM((levels, ring, lanes), jnp.float32)] * 2,
        input_output_aliases=aliases,
        cost_estimate=pl.CostEstimate(
            flops=count * 60, bytes_accessed=count * 8, transcendentals=0
        ),
        compiler_params=pltpu.CompilerParams(vmem_limit_bytes=VMEM_LIMIT),
        name="march",
    )(*operands)


def column_kernel(mix_ref, x_ref, base_ref, first_ref, factor):
    levels = x_ref.shape[1]

    def mix(k):
        return jnp.full((1, 128), mix_ref[k], jnp.float32)

    def wide(row, width):
        return jnp.tile(row, (1, width // 128))

    width = x_ref.shape[2]
    inverse = 1.0 / (1.0 + mix(1))
    factor[pl.ds(0, 1), :] = mix(1) * inverse
    first_ref[pl.ds(0, 1), :] = inverse
    for v in range(2):
        base_ref[v, pl.ds(0, 1), :] = x_ref[v, pl.ds(0, 1), :] * wide(inverse, width)

    def forward(k, carry):
        scaled, ones, heat, salt = carry
        low = mix(k)
        inv = 1.0 / (1.0 + low + mix(k + 1) - low * scaled)
        new_scaled = mix(k + 1) * inv
        factor[pl.ds(k, 1), :] = new_scaled
        ones = ones * low * inv
        first_ref[pl.ds(k, 1), :] = ones
        low_w, inv_w = wide(low, width), wide(inv, width)
        heat = (x_ref[0, pl.ds(k, 1), :] + low_w * heat) * inv_w
        salt = (x_ref[1, pl.ds(k, 1), :] + low_w * salt) * inv_w
        base_ref[0, pl.ds(k, 1), :] = heat
        base_ref[1, pl.ds(k, 1), :] = salt
        return new_scaled, ones, heat, salt

    lax.fori_loop(
        1,
        levels,
        forward,
        (
            factor[pl.ds(0, 1), :],
            inverse,
            base_ref[0, pl.ds(0, 1), :],
            base_ref[1, pl.ds(0, 1), :],
        ),
    )

    def backward(i, carry):
        ones, heat, salt = carry
        k = levels - 2 - i
        c = factor[pl.ds(k, 1), :]
        c_w = wide(c, width)
        ones = first_ref[pl.ds(k, 1), :] + c * ones
        heat = base_ref[0, pl.ds(k, 1), :] + c_w * heat
        salt = base_ref[1, pl.ds(k, 1), :] + c_w * salt
        first_ref[pl.ds(k, 1), :] = ones
        base_ref[0, pl.ds(k, 1), :] = heat
        base_ref[1, pl.ds(k, 1), :] = salt
        return ones, heat, salt

    lax.fori_loop(
        0,
        levels - 1,
        backward,
        (
            first_ref[pl.ds(levels - 1, 1), :],
            base_ref[0, pl.ds(levels - 1, 1), :],
            base_ref[1, pl.ds(levels - 1, 1), :],
        ),
    )


def two_parts(x):
    high = x.astype(jnp.bfloat16)
    return high, (x - high.astype(jnp.float32)).astype(jnp.bfloat16)


def remap_kernel(
    extent_ref, low_ref, mid_ref, high_ref, site_ref, share_ref, base_ref, first_ref,
    solved_ref, contrib_ref
):
    columns = site_ref.shape[1]
    crossings = site_ref.shape[0]
    rows = mid_ref.shape[1]
    index = lax.broadcasted_iota(jnp.int32, (128, columns), 0)
    parts = []
    pad = jnp.zeros((128 - 3 * rows, 128), jnp.float32)
    for v in range(2):
        table = jnp.concatenate([low_ref[v], mid_ref[v], high_ref[v], pad], axis=0).T
        parts.append(jnp.concatenate(two_parts(table), axis=1))
    tables = jnp.concatenate(parts, axis=0)
    forcing = [jnp.zeros((1, columns), jnp.float32)] * 2
    picks = []
    for n in range(crossings):
        site = site_ref[pl.ds(n, 1), :]
        row, lane = lax.shift_right_logical(site, 7), site & 127
        hot = jnp.where(index == row, 1.0, 0.0).astype(jnp.bfloat16)
        picks.append((hot, index == lane))
        picked = jnp.dot(
            tables, jnp.concatenate([hot, hot], axis=0), preferred_element_type=jnp.float32
        )
        weight = jnp.where(index == lane, share_ref[pl.ds(n, 1), :], 0.0)
        for v in range(2):
            forcing[v] = forcing[v] + jnp.sum(
                picked[128 * v : 128 * (v + 1)] * weight, axis=0, keepdims=True
            )
    slot = lax.broadcasted_iota(jnp.int32, (1, columns), 1)
    live = jnp.where(slot < extent_ref[0], 1.0, 0.0)
    answer = jnp.tile(first_ref[...], (1, columns // 128))
    heat = (base_ref[0] - 0.5 * forcing[0] * answer) * live
    solved_ref[0] = heat
    solved_ref[1] = (base_ref[1] + 0.5 * forcing[1] * answer) * live
    top = heat[:1]
    total = jnp.zeros((128, 512), jnp.float32)
    for n in range(crossings):
        hot, at_lane = picks[n]
        weight = share_ref[pl.ds(n, 1), :] * live
        pieces = []
        for value in (weight * top, weight):
            high = value.astype(jnp.bfloat16).astype(jnp.float32)
            for part in (high, value - high):
                pieces.append(jnp.where(at_lane, part, 0.0).astype(jnp.bfloat16))
        total = total + lax.dot_general(
            hot,
            jnp.concatenate(pieces, axis=0),
            (((1,), (1,)), ((), ())),
            preferred_element_type=jnp.float32,
        )
    for v in range(2):
        both = total[:, 256 * v : 256 * v + 128] + total[:, 256 * v + 128 : 256 * v + 256]
        for part in range(3):
            contrib_ref[part, v] = both[part * rows : (part + 1) * rows]


def local(
    prognostic_quantities,
    advective_ratio,
    horizontal_diffuse_ratio,
    upright_diffuse_ratio,
    transfer_coefficient,
    terrain_outer_warmth,
    earlier_marine_warmth,
    marine_indicator,
    marine_salinity_heat_vector,
    marine_layer_diffuse_ratio,
    group_active_extent,
    intersect_air_site,
    intersect_interpolation_share,
):
    kinds, levels, rows, lanes = prognostic_quantities.shape
    ring = rows + 8
    quarter = levels // 4
    fields = prognostic_quantities
    tile_count = lax.axis_size("tile")
    sec_index, tile_index = lax.axis_index("sec"), lax.axis_index("tile")
    sec = sec_index.astype(jnp.int32).reshape(1)

    share = marine_indicator.astype(jnp.float32)
    outer = share * earlier_marine_warmth + (1.0 - share) * terrain_outer_warmth
    moist = transfer_coefficient * (0.3 + 0.7 * share)
    none = jnp.zeros_like(outer)
    surface = jnp.stack(
        [
            jnp.stack([transfer_coefficient * outer, moist * (0.6 * outer), none, none, none]),
            jnp.stack(
                [transfer_coefficient, moist, none, transfer_coefficient, transfer_coefficient]
            ),
        ]
    )

    def row_halo(block):
        below, above = to_neighbours(block[..., :HALO, :], block[..., -HALO:, :], "tile")
        return ring_halo(below, above)

    def with_surface(rows_of):
        terms = jnp.swapaxes(surface[:, :, rows_of], 0, 1)
        return jnp.concatenate([fields[:, :, rows_of], terms], axis=1)

    below, above = to_neighbours(
        with_surface(slice(0, HALO)), with_surface(slice(rows - HALO, rows)), "tile"
    )
    halo = ring_halo(below[:, :levels], above[:, :levels])
    surface_halo = jnp.swapaxes(ring_halo(below[:, levels:], above[:, levels:]), 0, 1)

    chunk = 8
    own = pl.pallas_call(
        pack_kernel,
        grid=(quarter // chunk,),
        in_specs=[
            SMEM,
            pl.BlockSpec((kinds, 4, chunk, rows, lanes), lambda i: (0, 0, i, 0, 0)),
            VMEM,
        ],
        out_specs=pl.BlockSpec((quarter + 1, rows, lanes), lambda i: (0, 0, 0)),
        out_shape=jax.ShapeDtypeStruct((quarter + 1, rows, lanes), jnp.float32),
        compiler_params=pltpu.CompilerParams(vmem_limit_bytes=VMEM_LIMIT),
        name="pack",
    )(sec, fields.reshape(kinds, 4, quarter, rows, lanes), surface)
    swap = [(0, 1), (1, 0)]
    other = lax.ppermute(own, "sec", swap)
    own_halo = row_halo(own)
    other_halo = lax.ppermute(own_halo, "sec", swap)

    h, u = horizontal_diffuse_ratio, upright_diffuse_ratio
    ax, ay = 0.5 * advective_ratio[0], 0.5 * advective_ratio[1]
    by_level = jnp.stack([1.0 - 4.0 * h - 2.0 * u, h - ax, h + ax, h - ay, h + ay, u, u, u], axis=1)
    lane = jnp.arange(lanes)
    east_edge, west_edge = lane == lanes - 1, lane == 0
    is_west = sec_index == 0
    wide = jnp.broadcast_to(by_level[:, :, None], (levels, 8, lanes))
    which = jnp.arange(8)[None, :, None]
    beside = jnp.where(is_west, (h - ax)[:, None] * east_edge, (h + ax)[:, None] * west_edge)
    coef = jnp.where((which == 1) & east_edge, 0.0, wide)
    coef = jnp.where((which == 2) & west_edge, 0.0, coef)
    coef = jnp.where(which == 6, beside[:, None, :], coef)
    window_coef = jnp.repeat(by_level.reshape(4, quarter, 8).transpose(1, 2, 0), 32, axis=2)
    row = jnp.arange(ring)
    inside = (
        (row < rows)
        | ((row < rows + HALO) & (tile_index < tile_count - 1))
        | ((row >= ring - HALO) & (tile_index > 0))
    )
    mask = jnp.broadcast_to(inside.astype(jnp.float32)[:, None], (ring, lanes))

    ocean_levels, columns = marine_salinity_heat_vector.shape[1:]
    mix = jnp.pad(marine_layer_diffuse_ratio, (1, 1))
    base, first = call(
        column_kernel,
        in_specs=[SMEM, VMEM],
        out_specs=[VMEM, VMEM],
        out_shape=[
            jax.ShapeDtypeStruct(marine_salinity_heat_vector.shape, jnp.float32),
            jax.ShapeDtypeStruct((ocean_levels, 128), jnp.float32),
        ],
        scratch_shapes=[pltpu.VMEM((ocean_levels, 128), jnp.float32)],
        name="columns",
    )(mix, marine_salinity_heat_vector)

    seam = call(
        window_kernel,
        in_specs=[VMEM] * 6,
        out_specs=VMEM,
        out_shape=jax.ShapeDtypeStruct((STEPS, quarter, ring, lanes), jnp.float32),
        name="seam",
    )(own, other, own_halo, other_halo, window_coef, mask)

    common = (surface, surface_halo, seam, coef, mask)
    tracers, flux = march(GROUPS[0], sec, fields, halo, *common, None)
    block_axes = ("sec", "tile")
    flux_low, flux_high = to_neighbours(flux, flux, block_axes)
    (tracers,) = march(GROUPS[1], sec, fields, halo, *common, tracers)
    resolved, contrib = call(
        remap_kernel,
        in_specs=[SMEM] + [VMEM] * 7,
        out_specs=[VMEM, VMEM],
        out_shape=[
            jax.ShapeDtypeStruct(marine_salinity_heat_vector.shape, jnp.float32),
            jax.ShapeDtypeStruct((3, 2, rows, lanes), jnp.float32),
        ],
        name="remap",
    )(
        group_active_extent,
        flux_low,
        flux,
        flux_high,
        intersect_air_site,
        intersect_interpolation_share,
        base,
        first,
    )
    from_low, from_high = to_neighbours(contrib[0], contrib[2], block_axes)
    (tracers,) = march(GROUPS[2], sec, fields, halo, *common, tracers)
    gathered = contrib[1] + from_low + from_high
    upcoming = (gathered[0] + earlier_marine_warmth) / (gathered[1] + 1.0)
    return (tracers, resolved, upcoming)


def solution(mesh):
    return jax.shard_map(
        local,
        mesh=mesh,
        in_specs=(
            P(None, None, "tile", "sec"),
            P(),
            P(),
            P(),
            P("tile", "sec"),
            P("tile", "sec"),
            P("tile", "sec"),
            P("tile", "sec"),
            P(None, None, ("sec", "tile")),
            P(),
            P(("sec", "tile")),
            P(None, ("sec", "tile")),
            P(None, ("sec", "tile")),
        ),
        out_specs=(P(None, None, "tile", "sec"), P(None, None, ("sec", "tile")), P("tile", "sec")),
        check_vma=False,
    )
```

```python
import jax
import jax.numpy as jnp
from jax import lax
from jax.experimental import pallas as pl
from jax.experimental.pallas import tpu as pltpu
from jax.sharding import PartitionSpec as P

STEPS = 3
HALO = STEPS
WINDOW = 2 * HALO
VMEM_LIMIT = 48 * 1024 * 1024


def call(kernel, **kwargs):
    return pl.pallas_call(
        kernel,
        compiler_params=pltpu.CompilerParams(vmem_limit_bytes=VMEM_LIMIT),
        **kwargs,
    )


SMEM = pl.BlockSpec(memory_space=pltpu.SMEM)
VMEM = pl.BlockSpec(memory_space=pltpu.VMEM)


def to_neighbours(low_edge, high_edge, axis):
    count = lax.axis_size(axis)
    forward = [(i, i + 1) for i in range(count - 1)]
    backward = [(i + 1, i) for i in range(count - 1)]
    return lax.ppermute(high_edge, axis, forward), lax.ppermute(low_edge, axis, backward)


def ring_halo(below, above):
    gap = jnp.zeros(above.shape[:-2] + (8 - 2 * HALO, above.shape[-1]), above.dtype)
    return jnp.concatenate([above, gap, below], axis=-2)


def pack_kernel(sec_ref, x_ref, surface_ref, o_ref):
    step = pl.program_id(0)
    kinds, quarters, chunk, rows, lanes = x_ref.shape
    base = jnp.where(sec_ref[0] == 0, 128 - (128 - HALO), HALO)
    first = jnp.where(sec_ref[0] == 0, 0, HALO)
    lane = lax.broadcasted_iota(jnp.int32, (rows, lanes), 1)

    def placed(block, slot, total):
        at = 32 * slot[0] + WINDOW * slot[1]
        moved = pltpu.roll(block, lax.rem(base + at, 128), 1)
        inside = (lane >= at + first) & (lane < at + first + HALO)
        return jnp.where(inside, moved, total)

    def body(i, carry):
        total = jnp.zeros((rows, lanes), jnp.float32)
        for q in range(quarters):
            for v in range(kinds):
                total = placed(x_ref[v, q, i], (q, v), total)
        o_ref[step * chunk + i] = total
        return carry

    lax.fori_loop(0, chunk, body, 0, unroll=4)

    @pl.when(step == 0)
    def _():
        total = jnp.zeros((rows, lanes), jnp.float32)
        for q in range(2):
            for v in range(kinds):
                total = placed(surface_ref[q, v], (q, v), total)
        o_ref[o_ref.shape[0] - 1] = total


def window_kernel(own_ref, other_ref, own_halo_ref, other_halo_ref, coef_ref, mask_ref, h_ref):
    depth = h_ref.shape[1]
    rows = own_ref.shape[1]
    h_ref[0, :, :rows] = own_ref[:depth] + other_ref[:depth]
    h_ref[0, :, rows:] = own_halo_ref[:depth] + other_halo_ref[:depth]
    surface = jnp.concatenate(
        [
            own_ref[depth] + other_ref[depth],
            own_halo_ref[depth] + other_halo_ref[depth],
        ],
        axis=0,
    )
    lane = lax.broadcasted_iota(jnp.int32, surface.shape, 1)
    bottom = lane >= 96
    add_const = jnp.where(bottom, pltpu.roll(surface, 96, 1), 0.0)
    add_slope = jnp.where(bottom, pltpu.roll(surface, 64, 1), 0.0)
    ring = surface.shape[0]
    for s in range(STEPS - 1):

        def update(kk, above, below):
            f = h_ref[s, kk]
            c = [coef_ref[kk, pl.ds(n, 1), :] for n in range(6)]
            new = (
                c[0] * f
                + c[1] * pltpu.roll(f, 127, 1)
                + c[2] * pltpu.roll(f, 1, 1)
                + c[3] * pltpu.roll(f, ring - 1, 0)
                + c[4] * pltpu.roll(f, 1, 0)
                + c[5] * (above + below)
            )
            return f, new

        def store(kk, new):
            h_ref[s + 1, kk] = new * mask_ref[...]

        top, last = h_ref[s, 0], h_ref[s, depth - 1]
        _, new = update(0, jnp.where(lane < 32, top, pltpu.roll(last, 32, 1)), h_ref[s, 1])
        store(0, new)

        def body(kk, carry):
            _, new = update(kk, h_ref[s, kk - 1], h_ref[s, kk + 1])
            store(kk, new)
            return carry

        lax.fori_loop(1, depth - 1, body, 0, unroll=True)
        f, new = update(
            depth - 1, h_ref[s, depth - 2], jnp.where(bottom, last, pltpu.roll(top, 96, 1))
        )
        store(depth - 1, new + (add_const - add_slope * f))


def march_kernel(
    sec_ref, x_ref, halo_ref, surface_ref, h_ref, coef_ref, mask_ref, out_ref, flux_ref, s0, s1
):
    kind = pl.program_id(0)
    levels, rows = x_ref.shape[1:3]
    quarter = levels // 4
    ring = s0.shape[1]
    s0[:, :rows] = x_ref[0]
    s0[:, rows:] = halo_ref[0, :levels]
    is_west = sec_ref[0] == 0
    source = jnp.where(is_west, HALO, HALO - 1) + WINDOW * kind
    goal = jnp.where(is_west, 127, 0)
    halo_mask = mask_ref[pl.ds(rows, ring - rows), :]
    flux = None
    states = (s0, s1, s0)
    for s in range(STEPS):
        src = states[s]
        for q in range(4):
            shift = lax.rem(goal + 256 - source - 32 * q, 128)

            def body(kk, carry, src=src, q=q, shift=shift, s=s):
                k = q * quarter + kk
                f = src[k]
                above = src[jnp.maximum(k - 1, 0)]
                below = src[jnp.minimum(k + 1, levels - 1)]
                c = [coef_ref[k, pl.ds(n, 1), :] for n in range(7)]
                north = pltpu.roll(f, ring - 1, 0)
                south = pltpu.roll(f, 1, 0)
                beside = h_ref[s, kk]
                if s == STEPS - 1:
                    f, above, below, north, south, beside = (
                        a[:rows] for a in (f, above, below, north, south, beside)
                    )
                new = (
                    c[0] * f
                    + c[1] * pltpu.roll(f, 127, 1)
                    + c[2] * pltpu.roll(f, 1, 1)
                    + c[6] * pltpu.roll(beside, shift, 1)
                    + c[3] * north
                    + c[4] * south
                    + c[5] * (above + below)
                )
                if s == STEPS - 1:
                    out_ref[0, k] = new
                else:
                    dst = states[s + 1]
                    dst[k, pl.ds(0, rows), :] = new[:rows]
                    dst[k, pl.ds(rows, ring - rows), :] = new[rows:] * halo_mask
                return carry

            lax.fori_loop(0, quarter, body, 0, unroll=True)
        last = src[levels - 1]
        term = surface_ref[0, 0] - surface_ref[1, 0] * last[:rows]
        if s == STEPS - 1:
            out_ref[0, levels - 1] += term
        else:
            dst = states[s + 1]
            dst[levels - 1, pl.ds(0, rows), :] += term
            dst[levels - 1, pl.ds(rows, ring - rows), :] += halo_mask * (
                halo_ref[0, levels] - halo_ref[0, levels + 1] * last[rows:]
            )
        flux = term if flux is None else flux + term
    flux_ref[0] = flux


def march(sec, fields, halo, surface, seam, coef, mask):
    kinds, levels, rows, lanes = fields.shape
    block = pl.BlockSpec((1, levels, rows, lanes), lambda v: (v, 0, 0, 0))
    return pl.pallas_call(
        march_kernel,
        grid=(kinds,),
        in_specs=[
            SMEM,
            block,
            pl.BlockSpec((1, levels + 2, 8, lanes), lambda v: (v, 0, 0, 0)),
            pl.BlockSpec((2, 1, rows, lanes), lambda v: (0, v, 0, 0)),
            VMEM,
            VMEM,
            VMEM,
        ],
        out_specs=[block, pl.BlockSpec((1, rows, lanes), lambda v: (v, 0, 0))],
        out_shape=[
            jax.ShapeDtypeStruct(fields.shape, jnp.float32),
            jax.ShapeDtypeStruct((kinds, rows, lanes), jnp.float32),
        ],
        scratch_shapes=[pltpu.VMEM((levels, rows + 8, lanes), jnp.float32)] * 2,
        cost_estimate=pl.CostEstimate(
            flops=fields.size * 60, bytes_accessed=fields.size * 8, transcendentals=0
        ),
        compiler_params=pltpu.CompilerParams(vmem_limit_bytes=VMEM_LIMIT),
        name="march",
    )(sec, fields, halo, surface, seam, coef, mask)


def column_kernel(mix_ref, x_ref, base_ref, first_ref, factor):
    levels = x_ref.shape[1]

    def mix(k):
        return jnp.full((1, 128), mix_ref[k], jnp.float32)

    def wide(row, width):
        return jnp.tile(row, (1, width // 128))

    width = x_ref.shape[2]
    inverse = 1.0 / (1.0 + mix(1))
    factor[pl.ds(0, 1), :] = mix(1) * inverse
    first_ref[pl.ds(0, 1), :] = inverse
    for v in range(2):
        base_ref[v, pl.ds(0, 1), :] = x_ref[v, pl.ds(0, 1), :] * wide(inverse, width)

    def forward(k, carry):
        scaled, ones, heat, salt = carry
        low = mix(k)
        inv = 1.0 / (1.0 + low + mix(k + 1) - low * scaled)
        new_scaled = mix(k + 1) * inv
        factor[pl.ds(k, 1), :] = new_scaled
        ones = ones * low * inv
        first_ref[pl.ds(k, 1), :] = ones
        low_w, inv_w = wide(low, width), wide(inv, width)
        heat = (x_ref[0, pl.ds(k, 1), :] + low_w * heat) * inv_w
        salt = (x_ref[1, pl.ds(k, 1), :] + low_w * salt) * inv_w
        base_ref[0, pl.ds(k, 1), :] = heat
        base_ref[1, pl.ds(k, 1), :] = salt
        return new_scaled, ones, heat, salt

    lax.fori_loop(
        1,
        levels,
        forward,
        (
            factor[pl.ds(0, 1), :],
            inverse,
            base_ref[0, pl.ds(0, 1), :],
            base_ref[1, pl.ds(0, 1), :],
        ),
    )

    def backward(i, carry):
        ones, heat, salt = carry
        k = levels - 2 - i
        c = factor[pl.ds(k, 1), :]
        c_w = wide(c, width)
        ones = first_ref[pl.ds(k, 1), :] + c * ones
        heat = base_ref[0, pl.ds(k, 1), :] + c_w * heat
        salt = base_ref[1, pl.ds(k, 1), :] + c_w * salt
        first_ref[pl.ds(k, 1), :] = ones
        base_ref[0, pl.ds(k, 1), :] = heat
        base_ref[1, pl.ds(k, 1), :] = salt
        return ones, heat, salt

    lax.fori_loop(
        0,
        levels - 1,
        backward,
        (
            first_ref[pl.ds(levels - 1, 1), :],
            base_ref[0, pl.ds(levels - 1, 1), :],
            base_ref[1, pl.ds(levels - 1, 1), :],
        ),
    )


def two_parts(x):
    high = x.astype(jnp.bfloat16)
    return high, (x - high.astype(jnp.float32)).astype(jnp.bfloat16)


def exchange(sources, landing, send_sem, recv_sem, first, below, above):
    copies = []
    for n, device in enumerate((below, above)):
        copy = pltpu.make_async_remote_copy(
            src_ref=sources[n],
            dst_ref=landing.at[1 - n],
            send_sem=send_sem.at[first + n],
            recv_sem=recv_sem.at[first + 1 - n],
            device_id=device,
            device_id_type=pl.DeviceIdType.MESH,
        )
        copy.start()
        copies.append(copy)
    return copies


def remap_kernel(
    extent_ref, flux_ref, site_ref, share_ref, base_ref, first_ref, earlier_ref,
    solved_ref, warmth_ref, landed, outgoing, arrived, send_sem, recv_sem
):
    tiles = lax.axis_size("tile")
    blocks = tiles * lax.axis_size("sec")
    block = lax.axis_index("sec") * tiles + lax.axis_index("tile")
    near = []
    for away in (blocks - 1, 1):
        other = lax.rem(block + away, blocks)
        near.append((lax.div(other, tiles), lax.rem(other, tiles)))
    barrier = pltpu.get_barrier_semaphore()
    for device in near:
        pl.semaphore_signal(
            barrier, inc=1, device_id=device, device_id_type=pl.DeviceIdType.MESH
        )
    pl.semaphore_wait(barrier, 2)
    own = flux_ref.at[pl.ds(0, 2)]
    for copy in exchange((own, own), landed, send_sem, recv_sem, 0, *near):
        copy.wait()
    columns = site_ref.shape[1]
    crossings = site_ref.shape[0]
    rows = flux_ref.shape[1]
    index = lax.broadcasted_iota(jnp.int32, (128, columns), 0)
    parts = []
    pad = jnp.zeros((128 - 3 * rows, 128), jnp.float32)
    for v in range(2):
        table = jnp.concatenate([landed[0, v], flux_ref[v], landed[1, v], pad], axis=0).T
        parts.append(jnp.concatenate(two_parts(table), axis=1))
    tables = jnp.concatenate(parts, axis=0)
    forcing = [jnp.zeros((1, columns), jnp.float32)] * 2
    picks = []
    for n in range(crossings):
        site = site_ref[pl.ds(n, 1), :]
        row, lane = lax.shift_right_logical(site, 7), site & 127
        hot = jnp.where(index == row, 1.0, 0.0).astype(jnp.bfloat16)
        picks.append((hot, index == lane))
        picked = jnp.dot(
            tables, jnp.concatenate([hot, hot], axis=0), preferred_element_type=jnp.float32
        )
        weight = jnp.where(index == lane, share_ref[pl.ds(n, 1), :], 0.0)
        for v in range(2):
            forcing[v] = forcing[v] + jnp.sum(
                picked[128 * v : 128 * (v + 1)] * weight, axis=0, keepdims=True
            )
    slot = lax.broadcasted_iota(jnp.int32, (1, columns), 1)
    live = jnp.where(slot < extent_ref[0], 1.0, 0.0)
    answer = jnp.tile(first_ref[...], (1, columns // 128))
    heat = (base_ref[0] - 0.5 * forcing[0] * answer) * live
    solved_ref[0] = heat
    solved_ref[1] = (base_ref[1] + 0.5 * forcing[1] * answer) * live
    top = heat[:1]
    total = jnp.zeros((128, 512), jnp.float32)
    for n in range(crossings):
        hot, at_lane = picks[n]
        weight = share_ref[pl.ds(n, 1), :] * live
        pieces = []
        for value in (weight * top, weight):
            high = value.astype(jnp.bfloat16).astype(jnp.float32)
            for part in (high, value - high):
                pieces.append(jnp.where(at_lane, part, 0.0).astype(jnp.bfloat16))
        total = total + lax.dot_general(
            hot,
            jnp.concatenate(pieces, axis=0),
            (((1,), (1,)), ((), ())),
            preferred_element_type=jnp.float32,
        )
    mine = []
    for v in range(2):
        both = total[:, 256 * v : 256 * v + 128] + total[:, 256 * v + 128 : 256 * v + 256]
        outgoing[0, v] = both[:rows]
        mine.append(both[rows : 2 * rows])
        outgoing[1, v] = both[2 * rows : 3 * rows]
    sources = (outgoing.at[0], outgoing.at[1])
    for copy in exchange(sources, arrived, send_sem, recv_sem, 2, *near):
        copy.wait()
    heat_in, weight_in = (mine[v] + arrived[0, v] + arrived[1, v] for v in range(2))
    warmth_ref[...] = (heat_in + earlier_ref[...]) / (weight_in + 1.0)


def local(
    prognostic_quantities,
    advective_ratio,
    horizontal_diffuse_ratio,
    upright_diffuse_ratio,
    transfer_coefficient,
    terrain_outer_warmth,
    earlier_marine_warmth,
    marine_indicator,
    marine_salinity_heat_vector,
    marine_layer_diffuse_ratio,
    group_active_extent,
    intersect_air_site,
    intersect_interpolation_share,
):
    kinds, levels, rows, lanes = prognostic_quantities.shape
    ring = rows + 8
    quarter = levels // 4
    fields = prognostic_quantities
    tile_count = lax.axis_size("tile")
    sec_index, tile_index = lax.axis_index("sec"), lax.axis_index("tile")
    sec = sec_index.astype(jnp.int32).reshape(1)

    share = marine_indicator.astype(jnp.float32)
    outer = share * earlier_marine_warmth + (1.0 - share) * terrain_outer_warmth
    moist = transfer_coefficient * (0.3 + 0.7 * share)
    none = jnp.zeros_like(outer)
    surface = jnp.stack(
        [
            jnp.stack([transfer_coefficient * outer, moist * (0.6 * outer), none, none, none]),
            jnp.stack(
                [transfer_coefficient, moist, none, transfer_coefficient, transfer_coefficient]
            ),
        ]
    )

    def row_halo(block):
        below, above = to_neighbours(block[..., :HALO, :], block[..., -HALO:, :], "tile")
        return ring_halo(below, above)

    def with_surface(rows_of):
        terms = jnp.swapaxes(surface[:, :, rows_of], 0, 1)
        return jnp.concatenate([fields[:, :, rows_of], terms], axis=1)

    below, above = to_neighbours(
        with_surface(slice(0, HALO)), with_surface(slice(rows - HALO, rows)), "tile"
    )
    halo = ring_halo(below, above)

    chunk = 8
    own = pl.pallas_call(
        pack_kernel,
        grid=(quarter // chunk,),
        in_specs=[
            SMEM,
            pl.BlockSpec((kinds, 4, chunk, rows, lanes), lambda i: (0, 0, i, 0, 0)),
            VMEM,
        ],
        out_specs=pl.BlockSpec((quarter + 1, rows, lanes), lambda i: (0, 0, 0)),
        out_shape=jax.ShapeDtypeStruct((quarter + 1, rows, lanes), jnp.float32),
        compiler_params=pltpu.CompilerParams(vmem_limit_bytes=VMEM_LIMIT),
        name="pack",
    )(sec, fields.reshape(kinds, 4, quarter, rows, lanes), surface)
    swap = [(0, 1), (1, 0)]
    other = lax.ppermute(own, "sec", swap)
    own_halo = row_halo(own)
    other_halo = lax.ppermute(own_halo, "sec", swap)

    h, u = horizontal_diffuse_ratio, upright_diffuse_ratio
    ax, ay = 0.5 * advective_ratio[0], 0.5 * advective_ratio[1]
    by_level = jnp.stack([1.0 - 4.0 * h - 2.0 * u, h - ax, h + ax, h - ay, h + ay, u, u, u], axis=1)
    lane = jnp.arange(lanes)
    east_edge, west_edge = lane == lanes - 1, lane == 0
    is_west = sec_index == 0
    wide = jnp.broadcast_to(by_level[:, :, None], (levels, 8, lanes))
    which = jnp.arange(8)[None, :, None]
    beside = jnp.where(is_west, (h - ax)[:, None] * east_edge, (h + ax)[:, None] * west_edge)
    coef = jnp.where((which == 1) & east_edge, 0.0, wide)
    coef = jnp.where((which == 2) & west_edge, 0.0, coef)
    coef = jnp.where(which == 6, beside[:, None, :], coef)
    window_coef = jnp.repeat(by_level.reshape(4, quarter, 8).transpose(1, 2, 0), 32, axis=2)
    row = jnp.arange(ring)
    inside = (
        (row < rows)
        | ((row < rows + HALO) & (tile_index < tile_count - 1))
        | ((row >= ring - HALO) & (tile_index > 0))
    )
    mask = jnp.broadcast_to(inside.astype(jnp.float32)[:, None], (ring, lanes))

    ocean_levels, columns = marine_salinity_heat_vector.shape[1:]
    mix = jnp.pad(marine_layer_diffuse_ratio, (1, 1))
    base, first = call(
        column_kernel,
        in_specs=[SMEM, VMEM],
        out_specs=[VMEM, VMEM],
        out_shape=[
            jax.ShapeDtypeStruct(marine_salinity_heat_vector.shape, jnp.float32),
            jax.ShapeDtypeStruct((ocean_levels, 128), jnp.float32),
        ],
        scratch_shapes=[pltpu.VMEM((ocean_levels, 128), jnp.float32)],
        name="columns",
    )(mix, marine_salinity_heat_vector)

    seam = call(
        window_kernel,
        in_specs=[VMEM] * 6,
        out_specs=VMEM,
        out_shape=jax.ShapeDtypeStruct((STEPS, quarter, ring, lanes), jnp.float32),
        name="seam",
    )(own, other, own_halo, other_halo, window_coef, mask)

    tracers, flux = march(sec, fields, halo, surface, seam, coef, mask)
    pair = (2, 2, rows, lanes)
    resolved, upcoming = pl.pallas_call(
        remap_kernel,
        in_specs=[SMEM] + [VMEM] * 6,
        out_specs=[VMEM, VMEM],
        out_shape=[
            jax.ShapeDtypeStruct(marine_salinity_heat_vector.shape, jnp.float32),
            jax.ShapeDtypeStruct((rows, lanes), jnp.float32),
        ],
        scratch_shapes=[pltpu.VMEM(pair, jnp.float32)] * 3
        + [pltpu.SemaphoreType.DMA((4,)), pltpu.SemaphoreType.DMA((4,))],
        compiler_params=pltpu.CompilerParams(
            vmem_limit_bytes=VMEM_LIMIT, collective_id=0, has_side_effects=True
        ),
        name="remap",
    )(
        group_active_extent,
        flux,
        intersect_air_site,
        intersect_interpolation_share,
        base,
        first,
        earlier_marine_warmth,
    )
    return (tracers, resolved, upcoming)


def solution(mesh):
    return jax.shard_map(
        local,
        mesh=mesh,
        in_specs=(
            P(None, None, "tile", "sec"),
            P(),
            P(),
            P(),
            P("tile", "sec"),
            P("tile", "sec"),
            P("tile", "sec"),
            P("tile", "sec"),
            P(None, None, ("sec", "tile")),
            P(),
            P(("sec", "tile")),
            P(None, ("sec", "tile")),
            P(None, ("sec", "tile")),
        ),
        out_specs=(P(None, None, "tile", "sec"), P(None, None, ("sec", "tile")), P("tile", "sec")),
        check_vma=False,
    )
```
